32 devices in a mesh: row: 4 (over z), col: 8 (over y, x, core).
Axes of the slice: x: 2, y: 2, z: 4, core: 2. Of those that a mesh axis runs over, the one named last changes fastest.
Arguments:
- source_tiles: bfloat16 [4, 8, 1024, 128], P('row', 'col'), may hold values from -6 to 6
- requests: int32 [4, 8, 8, 256], P('row', 'col'), may hold values from 0 to 1023
- stencil: int32 [128, 256, 4], P('row', 'col'), may hold values from 0 to 2047, as said below
- regrid_weight: float32 [128, 256, 4], P('row', 'col'), may hold values from 0.1 to 0.6
- w_in: bfloat16 [3, 3, 64, 128], replicated, may hold values from -0.4375 to 0.4375
- w_enc: bfloat16 [3, 3, 128, 128], replicated, may hold values from -0.3125 to 0.3125
- w_mid_first: bfloat16 [3, 3, 128, 128], replicated, may hold values from -0.3125 to 0.3125
- w_mid_second: bfloat16 [3, 3, 128, 128], replicated, may hold values from -0.3125 to 0.3125
- w_dec_first: bfloat16 [3, 3, 256, 128], replicated, may hold values from -0.21875 to 0.21875
- w_dec_second: bfloat16 [3, 3, 128, 128], replicated, may hold values from -0.3125 to 0.3125
- w_out: bfloat16 [128, 64], replicated, may hold values from -0.75 to 0.75
Outputs:
- forecast: bfloat16 [128, 256, 2, 64], P('row', 'col')
The draws below stay inside these ranges and needn't reach their ends.
Inputs may be any that keep to these rules, and one draw needn't show every extreme that they name: `stencil`: within each device's 32 x 32 block of target cells, every slot 0 to 2047 appears at least once among the entries.
All inputs are finite; a program needn't handle non-finite values.
Results may differ from the reference program's by a relative error of at most 0.017.
Values may be sent and summed in bfloat16 or wider, within the bound.
A program may use at most 64 MiB of HBM per device.

```python
import jax
import jax.numpy as jnp
from jax import lax

FIELDS = 64
CH = 128
K = 4
B = 2
TH = 32
TW = 32
SRC = 1024
CAP = 256
SLOTS = 2048
NY = 128
NX = 256
N_ROW = 4
N_COL = 8


def shuffle_reads(tile_key):
    return jax.random.permutation(tile_key, TH * TW * K).astype(jnp.int32)


def draw_stencil(key, part):
    tile_count = N_ROW * N_COL
    tile_reads = TH * TW * K
    tile_keys = jax.random.split(jax.random.fold_in(key, 11), tile_count)
    slot_order = jax.vmap(shuffle_reads)(tile_keys)
    spare_slots = jax.random.randint(jax.random.fold_in(key, 12), (tile_count, tile_reads), 0, SLOTS, dtype=jnp.int32)
    values = jnp.where(slot_order < SLOTS, slot_order, spare_slots)
    values = values.reshape(N_ROW, N_COL, TH, TW, K)
    values = jnp.transpose(values, (0, 2, 1, 3, 4)).reshape(NY, NX, K)
    return values.astype(jnp.int32)


def touch_ends(values, rng, least, top_value):
    extent = values.shape
    place = [jax.random.randint(jax.random.fold_in(rng, axis), (), 0, extent[axis]) for axis in range(len(extent))]
    values = values.at[tuple(place)].set(least)
    longest = extent.index(max(extent))
    place[longest] = (place[longest] + 1) % extent[longest]
    return values.at[tuple(place)].set(top_value)


def block_levels(stream_key, dims, cuts, smallest, largest):
    factor_of = 1.0
    for dim, parts in cuts:
        steps = jax.random.uniform(jax.random.fold_in(jax.random.fold_in(stream_key, 6), dim), (parts,), jnp.float32, smallest / len(cuts), largest / len(cuts))
        factor_of = factor_of * jnp.repeat(jnp.exp(steps), dims[dim] // parts).reshape((-1,) + (1,) * (len(dims) - 1 - dim))
    return factor_of


def normal_values(own_key, dims, scale, reach, pieces=(), kind=jnp.bfloat16):
    entries = scale * jax.random.normal(own_key, dims, jnp.float32)
    if pieces:
        entries = entries * block_levels(own_key, dims, pieces, -0.22, 0.18)
    return jnp.clip(entries, -reach, reach).astype(kind)


def setup_inputs(seed: int = 0) -> dict:
    seeds = jax.random.split(jax.random.key(seed), 12)
    return {
        "source_tiles": normal_values(seeds[0], (N_ROW, N_COL, SRC, B * FIELDS), 1.0, 6.0, ((0, 4), (1, 8))),
        "requests": touch_ends(jax.random.randint(seeds[1], (N_ROW, N_COL, N_COL, CAP), 0, SRC), jax.random.fold_in(seeds[1], 1), 0, SRC - 1).astype(jnp.int32),
        "stencil": draw_stencil(jax.random.fold_in(seeds[11], 71), 0),
        "regrid_weight": jnp.clip(0.1 + 0.5 * jax.random.uniform(seeds[3], (NY, NX, K), jnp.float32) ** block_levels(seeds[3], (NY, NX, K), ((0, 4), (1, 8)), -0.2, 0.2), 0.1, 0.6),
        "w_in": normal_values(seeds[4], (3, 3, FIELDS, CH), (3 * FIELDS) ** -0.5, 0.4375),
        "w_enc": normal_values(seeds[5], (3, 3, CH, CH), (3 * CH) ** -0.5, 0.3125),
        "w_mid_first": normal_values(seeds[6], (3, 3, CH, CH), (3 * CH) ** -0.5, 0.3125),
        "w_mid_second": normal_values(seeds[7], (3, 3, CH, CH), (3 * CH) ** -0.5, 0.3125),
        "w_dec_first": normal_values(seeds[8], (3, 3, 2 * CH, CH), (6 * CH) ** -0.5, 0.21875),
        "w_dec_second": normal_values(seeds[9], (3, 3, CH, CH), (3 * CH) ** -0.5, 0.3125),
        "w_out": normal_values(seeds[10], (CH, FIELDS), (CH // 2) ** -0.5, 0.75),
    }


def conv_same(values, weight):
    padded = jnp.pad(values, ((0, 0), (1, 1), (0, 0), (0, 0)), mode="wrap")
    padded = jnp.pad(padded, ((1, 1), (0, 0), (0, 0), (0, 0)))
    inputs = jnp.transpose(padded, (2, 0, 1, 3)).astype(jnp.float32)
    result = lax.conv_general_dilated(inputs, weight.astype(jnp.float32), (1, 1), "VALID", dimension_numbers=("NHWC", "HWIO", "NHWC"), precision=lax.Precision.HIGHEST)
    return jnp.transpose(result, (1, 2, 0, 3))


def layer(values, weight):
    return jax.nn.silu(conv_same(values, weight)).astype(jnp.bfloat16)


def reference(source_tiles, requests, stencil, regrid_weight, w_in, w_enc, w_mid_first, w_mid_second, w_dec_first, w_dec_second, w_out):
    def band_rows(block):
        tiles_band = source_tiles[block]
        wanted = requests[block]
        senders = jnp.arange(N_COL, dtype=jnp.int32)[None, :, None]
        buffer = tiles_band[senders, wanted]
        flattened = buffer.reshape(N_COL * SLOTS, B * FIELDS)
        start = (block * TH).astype(jnp.int32)
        band_stencil = lax.dynamic_slice_in_dim(stencil, start, TH, 0)
        band_weight = lax.dynamic_slice_in_dim(regrid_weight, start, TH, 0)
        owner = (jnp.arange(NX, dtype=jnp.int32) // TW)[None, :, None]
        picked = flattened[owner * SLOTS + band_stencil]
        total = jnp.sum(picked.astype(jnp.float32) * band_weight[..., None], axis=2)
        return total.astype(jnp.bfloat16)

    bands = lax.map(band_rows, jnp.arange(N_ROW, dtype=jnp.int32))
    regridded = bands.reshape(NY, NX, B, FIELDS)
    first = layer(regridded, w_in)
    skip = layer(first, w_enc)
    pooled = skip.astype(jnp.float32).reshape(NY // 2, 2, NX // 2, 2, B, CH).mean(axis=(1, 3)).astype(jnp.bfloat16)
    middle = layer(pooled, w_mid_first)
    coarse = layer(middle, w_mid_second)
    upsampled = jnp.repeat(jnp.repeat(coarse, 2, axis=0), 2, axis=1)
    joined = jnp.concatenate([upsampled, skip], axis=-1)
    decoded = layer(layer(joined, w_dec_first), w_dec_second)
    result = jnp.dot(decoded.reshape(-1, CH), w_out, preferred_element_type=jnp.float32)
    return result.reshape(NY, NX, B, FIELDS).astype(jnp.bfloat16)
```

```python
import functools

import jax
import jax.numpy as jnp
from jax import lax
from jax.experimental import pallas as pl
from jax.experimental.pallas import tpu as pltpu
from jax.sharding import PartitionSpec as P

FIELDS = 64
CH = 128
HALO = 8


def silu(a):
    return a * (0.5 + 0.5 * jnp.tanh(0.5 * a))


def unet_kernel(
    tile_rows, tile_cols, p_ref, w_in, w_enc, w_m1, w_m2, w_d1, w_d2, w_out, out_ref,
    first, skip, pooled, middle, up, dec1, tmp, c_in, c_enc, c_m1, c_m2, c_d1u, c_d1s, c_d2, c_out,
):
    wide = tile_cols + 2 * HALO
    half = wide // 2
    row = lax.axis_index("row")
    at_top = row == 0
    at_bottom = row == lax.axis_size("row") - 1
    f32, bf16 = jnp.float32, jnp.bfloat16

    c_in[...] = jnp.zeros_like(c_in)
    c_out[...] = jnp.zeros_like(c_out)
    for b in range(2):
        c_out[b * CH : (b + 1) * CH, b * FIELDS : (b + 1) * FIELDS] = w_out[...]
    for dy in range(3):
        for dx in range(3):
            rows = slice(dy * CH, (dy + 1) * CH)
            cols = slice(dx * CH, (dx + 1) * CH)
            for b in range(2):
                c_in[b, dy * CH + b * FIELDS : dy * CH + (b + 1) * FIELDS, cols] = w_in[dy, dx]
            c_enc[rows, cols] = w_enc[dy, dx]
            c_m1[rows, cols] = w_m1[dy, dx]
            c_m2[rows, cols] = w_m2[dy, dx]
            c_d1u[rows, cols] = w_d1[dy, dx, :CH]
            c_d1s[rows, cols] = w_d1[dy, dx, CH:]
            c_d2[rows, cols] = w_d2[dy, dx]

    def conv(sources, width, chunk_rows, start):
        size = chunk_rows * width
        u = None
        for load, weight, offset in sources:
            windows = [
                load(pl.multiple_of(start + (offset + dy) * width, 8), size).astype(bf16)
                for dy in range(3)
            ]
            part = jnp.dot(
                jnp.concatenate(windows, axis=1), weight[...], preferred_element_type=f32
            )
            u = part if u is None else u + part
        return silu(
            u[:, CH : 2 * CH]
            + pltpu.roll(u[:, :CH], 1, 0)
            + pltpu.roll(u[:, 2 * CH :], size - 1, 0)
        )

    def per_chunk(height, chunk_rows, width, step):
        chunks = height // chunk_rows

        @pl.loop(0, 2 * chunks)
        def _(i):
            b = i // chunks
            start = pl.multiple_of((i % chunks) * (chunk_rows * width), 8)
            step(b, start)

    def clear(ref, depth, inner, width):
        @pl.when(at_top)
        def _():
            ref[:, : depth * width] = jnp.zeros((2, depth * width, CH), ref.dtype)

        @pl.when(at_bottom)
        def _():
            ref[:, (depth + inner) * width :] = jnp.zeros((2, depth * width, CH), ref.dtype)

    def reader(ref, b):
        return lambda start, size: ref[b, pl.ds(start, size), :]

    h_first = tile_rows + 14
    h_skip = tile_rows + 12
    h_pool = h_skip // 2
    h_mid = h_pool - 2
    h_coarse = h_mid - 2
    h_dec1 = tile_rows + 2

    def first_step(b, start):
        chunk = h_first // 2
        value = conv(
            [(lambda s, n: p_ref[pl.ds(s, n), :], c_in.at[b], 0)], wide, chunk, start
        )
        first[b, pl.ds(start, chunk * wide), :] = value.astype(bf16)

    per_chunk(h_first, h_first // 2, wide, first_step)
    clear(first, 7, tile_rows, wide)

    def skip_step(b, start):
        chunk = h_skip // 2
        value = conv([(reader(first, b), c_enc, 0)], wide, chunk, start)
        skip[b, pl.ds(start, chunk * wide), :] = value.astype(bf16)

    per_chunk(h_skip, h_skip // 2, wide, skip_step)
    clear(skip, 6, tile_rows, wide)

    @pl.loop(0, 2)
    def _(b):
        s = skip[b].astype(f32).reshape(h_pool, 2 * wide, CH)
        tmp[: h_pool * wide, :] = (s[:, :wide] + s[:, wide:]).reshape(h_pool * wide, CH)
        total = (
            tmp[pl.ds(0, h_pool * half, stride=2), :] + tmp[pl.ds(1, h_pool * half, stride=2), :]
        )
        pooled[b] = (total * 0.25).astype(bf16).astype(f32)

    def mid_step(b, start):
        value = conv([(reader(pooled, b), c_m1, 0)], half, h_mid, start)
        middle[b, pl.ds(start, h_mid * half), :] = value.astype(bf16).astype(f32)

    per_chunk(h_mid, h_mid, half, mid_step)
    clear(middle, 2, tile_rows // 2, half)

    @pl.loop(0, 2)
    def _(b):
        value = conv([(reader(middle, b), c_m2, 0)], half, h_coarse, 0)
        size = h_coarse * half
        tmp[pl.ds(0, size, stride=2), :] = value
        tmp[pl.ds(1, size, stride=2), :] = value
        v = tmp[: h_coarse * wide, :].astype(bf16).reshape(h_coarse, 1, wide, CH)
        up[b] = jnp.broadcast_to(v, (h_coarse, 2, wide, CH)).reshape(2 * h_coarse * wide, CH)

    clear(up, 2, tile_rows, wide)

    def dec1_step(b, start):
        chunk = h_dec1 // 2
        value = conv(
            [(reader(up, b), c_d1u, 0), (reader(skip, b), c_d1s, 4)], wide, chunk, start
        )
        dec1[b, pl.ds(start, chunk * wide), :] = value.astype(bf16)

    per_chunk(h_dec1, h_dec1 // 2, wide, dec1_step)
    clear(dec1, 1, tile_rows, wide)

    chunk = tile_rows // 2

    @pl.loop(0, 2)
    def _(i):
        start = pl.multiple_of(i * (chunk * wide), 8)
        both = []
        for b in range(2):
            value = conv([(reader(dec1, b), c_d2, 0)], wide, chunk, start)
            value = value.reshape(chunk, wide, CH)[:, HALO : HALO + tile_cols]
            both.append(value.reshape(chunk * tile_cols, CH).astype(bf16))
        result = jnp.dot(
            jnp.concatenate(both, axis=1), c_out[...], preferred_element_type=f32
        )
        place = pl.multiple_of(i * (chunk * tile_cols), 8)
        out_ref[pl.ds(place, chunk * tile_cols), :] = result.astype(bf16)


def unet(padded, tile_rows, tile_cols, weights):
    wide = tile_cols + 2 * HALO
    half = wide // 2
    f32, bf16 = jnp.float32, jnp.bfloat16
    square = pltpu.VMEM((3 * CH, 3 * CH), bf16)
    scratch = [
        pltpu.VMEM((2, (tile_rows + 14) * wide, CH), bf16),
        pltpu.VMEM((2, (tile_rows + 12) * wide, CH), bf16),
        pltpu.VMEM((2, (tile_rows // 2 + 6) * half, CH), f32),
        pltpu.VMEM((2, (tile_rows // 2 + 4) * half, CH), f32),
        pltpu.VMEM((2, (tile_rows + 4) * wide, CH), bf16),
        pltpu.VMEM((2, (tile_rows + 2) * wide, CH), bf16),
        pltpu.VMEM(((tile_rows // 2 + 6) * wide, CH), f32),
        pltpu.VMEM((2, 3 * CH, 3 * CH), bf16),
        square, square, square, square, square, square,
        pltpu.VMEM((2 * CH, 2 * FIELDS), bf16),
    ]
    return pl.pallas_call(
        functools.partial(unet_kernel, tile_rows, tile_cols),
        out_shape=jax.ShapeDtypeStruct((tile_rows * tile_cols, 2 * FIELDS), bf16),
        in_specs=[pl.BlockSpec(memory_space=pltpu.VMEM)] * 8,
        out_specs=pl.BlockSpec(memory_space=pltpu.VMEM),
        scratch_shapes=scratch,
        compiler_params=pltpu.CompilerParams(vmem_limit_bytes=44 * 1024 * 1024),
        cost_estimate=pl.CostEstimate(
            flops=6 * 10**9, bytes_accessed=4 * 10**6, transcendentals=2 * 10**6
        ),
    )(padded, *weights)


def with_halo(x, sides, width):
    for axis, dim in sides:
        devices, length = (lax.axis_size(axis), x.shape[dim])
        up = [(i, (i + 1) % devices) for i in range(devices)]
        down = [(j, i) for i, j in up]
        last = lax.slice_in_dim(x, length - width, length, axis=dim)
        leading = lax.slice_in_dim(x, 0, width, axis=dim)
        before = lax.ppermute(last, axis, up)
        after = lax.ppermute(leading, axis, down)
        x = jnp.concatenate([before, x, after], axis=dim)
    return x


def rim_clear(padded, depth, rows_dev):
    global_rows = (
        lax.axis_index("row") * rows_dev + jnp.arange(padded.shape[0], dtype=jnp.int32) - depth
    )
    inside = (global_rows >= 0) & (global_rows < lax.axis_size("row") * rows_dev)
    return jnp.where(inside[:, None, None], padded, jnp.zeros_like(padded))


def body(source_tiles, requests, stencil, regrid_weight, *weights):
    tile_rows = stencil.shape[0]
    tile_cols = stencil.shape[1]
    columns = source_tiles.shape[3]
    cells = source_tiles.shape[2]
    groups = requests.shape[2]
    capacity = requests.shape[3]
    wanted = requests.reshape(groups, capacity)
    global_ids = (jnp.arange(groups, dtype=jnp.int32)[:, None] * cells + wanted).reshape(-1)
    flattened = lax.all_gather(source_tiles, "col", axis=1, tiled=True).reshape(-1, columns)
    buffer = flattened[global_ids]
    picked = buffer[stencil]
    regridded = jnp.sum(picked.astype(jnp.float32) * regrid_weight[..., None], axis=2).astype(
        jnp.bfloat16
    )
    padded = rim_clear(with_halo(regridded, (("row", 0), ("col", 1)), HALO), HALO, tile_rows)
    result = unet(padded.reshape(-1, columns), tile_rows, tile_cols, weights)
    return result.reshape(tile_rows, tile_cols, 2, FIELDS)


def solution(mesh):
    placed = (P("row", "col", None, None),) * 2 + (P("row", "col", None),) * 2 + (P(),) * 7
    return jax.shard_map(
        body, mesh=mesh, in_specs=placed, out_specs=P("row", "col", None, None), check_vma=False
    )
```

```python
import functools

import jax
import jax.numpy as jnp
from jax import lax
from jax.experimental import pallas as pl
from jax.experimental.pallas import tpu as pltpu
from jax.sharding import PartitionSpec as P

FIELDS = 64
CH = 128
HALO = 8


def silu(a):
    return a * (0.5 + 0.5 * jnp.tanh(0.5 * a))


def unet_kernel(
    tile_rows, tile_cols, p_ref, w_in, w_enc, w_m1, w_m2, w_d1, w_d2, w_out, out_ref,
    first, skip, pooled, middle, up, dec1, tmp, c_in, c_enc, c_m1, c_m2, c_d1u, c_d1s, c_d2, c_out,
):
    wide = tile_cols + 2 * HALO
    half = wide // 2
    row = lax.axis_index("row")
    at_top = row == 0
    at_bottom = row == lax.axis_size("row") - 1
    f32, bf16 = jnp.float32, jnp.bfloat16

    c_in[...] = jnp.zeros_like(c_in)
    c_out[...] = jnp.zeros_like(c_out)
    for b in range(2):
        c_out[b * CH : (b + 1) * CH, b * FIELDS : (b + 1) * FIELDS] = w_out[...]
    for dy in range(3):
        for dx in range(3):
            rows = slice(dy * CH, (dy + 1) * CH)
            cols = slice(dx * CH, (dx + 1) * CH)
            for b in range(2):
                c_in[b, dy * CH + b * FIELDS : dy * CH + (b + 1) * FIELDS, cols] = w_in[dy, dx]
            c_enc[rows, cols] = w_enc[dy, dx]
            c_m1[rows, cols] = w_m1[dy, dx]
            c_m2[rows, cols] = w_m2[dy, dx]
            c_d1u[rows, cols] = w_d1[dy, dx, :CH]
            c_d1s[rows, cols] = w_d1[dy, dx, CH:]
            c_d2[rows, cols] = w_d2[dy, dx]

    def conv(sources, width, chunk_rows, start):
        size = chunk_rows * width
        u = None
        for load, weight, offset in sources:
            windows = [
                load(pl.multiple_of(start + (offset + dy) * width, 8), size).astype(bf16)
                for dy in range(3)
            ]
            part = jnp.dot(
                jnp.concatenate(windows, axis=1), weight[...], preferred_element_type=f32
            )
            u = part if u is None else u + part
        return silu(
            u[:, CH : 2 * CH]
            + pltpu.roll(u[:, :CH], 1, 0)
            + pltpu.roll(u[:, 2 * CH :], size - 1, 0)
        )

    def per_chunk(height, chunk_rows, width, step):
        chunks = height // chunk_rows

        @pl.loop(0, 2 * chunks)
        def _(i):
            b = i // chunks
            start = pl.multiple_of((i % chunks) * (chunk_rows * width), 8)
            step(b, start)

    def clear(ref, depth, inner, width):
        @pl.when(at_top)
        def _():
            ref[:, : depth * width] = jnp.zeros((2, depth * width, CH), ref.dtype)

        @pl.when(at_bottom)
        def _():
            ref[:, (depth + inner) * width :] = jnp.zeros((2, depth * width, CH), ref.dtype)

    def reader(ref, b):
        return lambda start, size: ref[b, pl.ds(start, size), :]

    h_first = tile_rows + 14
    h_skip = tile_rows + 12
    h_pool = h_skip // 2
    h_mid = h_pool - 2
    h_coarse = h_mid - 2
    h_dec1 = tile_rows + 2

    def first_step(b, start):
        chunk = h_first // 2
        value = conv(
            [(lambda s, n: p_ref[pl.ds(s, n), :], c_in.at[b], 0)], wide, chunk, start
        )
        first[b, pl.ds(start, chunk * wide), :] = value.astype(bf16)

    per_chunk(h_first, h_first // 2, wide, first_step)
    clear(first, 7, tile_rows, wide)

    def skip_step(b, start):
        chunk = h_skip // 2
        value = conv([(reader(first, b), c_enc, 0)], wide, chunk, start)
        skip[b, pl.ds(start, chunk * wide), :] = value.astype(bf16)

    per_chunk(h_skip, h_skip // 2, wide, skip_step)
    clear(skip, 6, tile_rows, wide)

    @pl.loop(0, 2)
    def _(b):
        s = skip[b].astype(f32).reshape(h_pool, 2 * wide, CH)
        tmp[: h_pool * wide, :] = (s[:, :wide] + s[:, wide:]).reshape(h_pool * wide, CH)
        total = (
            tmp[pl.ds(0, h_pool * half, stride=2), :] + tmp[pl.ds(1, h_pool * half, stride=2), :]
        )
        pooled[b] = (total * 0.25).astype(bf16).astype(f32)

    def mid_step(b, start):
        value = conv([(reader(pooled, b), c_m1, 0)], half, h_mid, start)
        middle[b, pl.ds(start, h_mid * half), :] = value.astype(bf16).astype(f32)

    per_chunk(h_mid, h_mid, half, mid_step)
    clear(middle, 2, tile_rows // 2, half)

    @pl.loop(0, 2)
    def _(b):
        value = conv([(reader(middle, b), c_m2, 0)], half, h_coarse, 0)
        size = h_coarse * half
        tmp[pl.ds(0, size, stride=2), :] = value
        tmp[pl.ds(1, size, stride=2), :] = value
        v = tmp[: h_coarse * wide, :].astype(bf16).reshape(h_coarse, 1, wide, CH)
        up[b] = jnp.broadcast_to(v, (h_coarse, 2, wide, CH)).reshape(2 * h_coarse * wide, CH)

    clear(up, 2, tile_rows, wide)

    def dec1_step(b, start):
        chunk = h_dec1 // 2
        value = conv(
            [(reader(up, b), c_d1u, 0), (reader(skip, b), c_d1s, 4)], wide, chunk, start
        )
        dec1[b, pl.ds(start, chunk * wide), :] = value.astype(bf16)

    per_chunk(h_dec1, h_dec1 // 2, wide, dec1_step)
    clear(dec1, 1, tile_rows, wide)

    chunk = tile_rows // 2

    @pl.loop(0, 2)
    def _(i):
        start = pl.multiple_of(i * (chunk * wide), 8)
        both = []
        for b in range(2):
            value = conv([(reader(dec1, b), c_d2, 0)], wide, chunk, start)
            value = value.reshape(chunk, wide, CH)[:, HALO : HALO + tile_cols]
            both.append(value.reshape(chunk * tile_cols, CH).astype(bf16))
        result = jnp.dot(
            jnp.concatenate(both, axis=1), c_out[...], preferred_element_type=f32
        )
        place = pl.multiple_of(i * (chunk * tile_cols), 8)
        out_ref[pl.ds(place, chunk * tile_cols), :] = result.astype(bf16)


def unet(padded, tile_rows, tile_cols, weights):
    wide = tile_cols + 2 * HALO
    half = wide // 2
    f32, bf16 = jnp.float32, jnp.bfloat16
    square = pltpu.VMEM((3 * CH, 3 * CH), bf16)
    scratch = [
        pltpu.VMEM((2, (tile_rows + 14) * wide, CH), bf16),
        pltpu.VMEM((2, (tile_rows + 12) * wide, CH), bf16),
        pltpu.VMEM((2, (tile_rows // 2 + 6) * half, CH), f32),
        pltpu.VMEM((2, (tile_rows // 2 + 4) * half, CH), f32),
        pltpu.VMEM((2, (tile_rows + 4) * wide, CH), bf16),
        pltpu.VMEM((2, (tile_rows + 2) * wide, CH), bf16),
        pltpu.VMEM(((tile_rows // 2 + 6) * wide, CH), f32),
        pltpu.VMEM((2, 3 * CH, 3 * CH), bf16),
        square, square, square, square, square, square,
        pltpu.VMEM((2 * CH, 2 * FIELDS), bf16),
    ]
    return pl.pallas_call(
        functools.partial(unet_kernel, tile_rows, tile_cols),
        out_shape=jax.ShapeDtypeStruct((tile_rows * tile_cols, 2 * FIELDS), bf16),
        in_specs=[pl.BlockSpec(memory_space=pltpu.VMEM)] * 8,
        out_specs=pl.BlockSpec(memory_space=pltpu.VMEM),
        scratch_shapes=scratch,
        compiler_params=pltpu.CompilerParams(vmem_limit_bytes=44 * 1024 * 1024),
        cost_estimate=pl.CostEstimate(
            flops=6 * 10**9, bytes_accessed=4 * 10**6, transcendentals=2 * 10**6
        ),
    )(padded, *weights)


MESH = pl.DeviceIdType.MESH


def regrid_kernel(
    tile_rows, tile_cols, src_ref, req_ref, sten_ref, wgt_ref, out_ref,
    reqs, src_t, mix, outbox, inbox, acc, pad,
    req_send, req_recv, box_send, box_recv, halo_send, halo_recv,
):
    f32, bf16 = jnp.float32, jnp.bfloat16
    row, me = lax.axis_index("row"), lax.axis_index("col")
    n_row, n = lax.axis_size("row"), lax.axis_size("col")
    cap = req_ref.shape[1]
    cells = src_ref.shape[0]
    spots = tile_rows * tile_cols
    has_up, has_down = row > 0, row < n_row - 1
    blocks = tile_cols // HALO
    edge = HALO * HALO
    inner = tile_rows * HALO

    barrier = pltpu.get_barrier_semaphore()

    def greet(r, c):
        pl.semaphore_signal(
            barrier, inc=1, device_id=(r, lax.rem(c + n, n)), device_id_type=MESH
        )

    @pl.loop(1, n)
    def _(step):
        greet(row, me + step)

    @pl.when(has_up)
    def _():
        for d in (-1, 0, 1):
            greet(row - 1, me + d)

    @pl.when(has_down)
    def _():
        for d in (-1, 0, 1):
            greet(row + 1, me + d)

    rows_beside = jnp.minimum(row, 1) + jnp.minimum(n_row - 1 - row, 1)
    pl.semaphore_wait(barrier, n - 1 + 3 * rows_beside)

    def ask(step, sender):
        return pltpu.make_async_remote_copy(
            src_ref=req_ref,
            dst_ref=reqs.at[sender],
            send_sem=req_send.at[step],
            recv_sem=req_recv.at[sender],
            device_id=(row, lax.rem(me + step, n)),
            device_id_type=MESH,
        )

    @pl.loop(1, n)
    def _(step):
        ask(step, me).start()

    reqs[me] = req_ref[...]
    src_t[...] = src_ref[...].astype(f32).T.astype(bf16)

    def mix_block(j):
        slots = lax.broadcasted_iota(jnp.int32, (cap, spots), 0)
        total = None
        for k in range(sten_ref.shape[0]):
            hit = slots == sten_ref[k : k + 1, :] - j * cap
            part = jnp.where(hit, wgt_ref[k : k + 1, :], 0.0)
            total = part if total is None else total + part
        mix[j] = total.astype(bf16)

    @pl.loop(0, n // 2)
    def _(j):
        mix_block(j)

    def picked(dest):
        ids = lax.broadcasted_iota(jnp.int32, (cells, cap), 0)
        hot = jnp.where(ids == reqs[dest, pl.ds(me, 1), :], 1.0, 0.0).astype(bf16)
        return jnp.dot(src_t[...], hot, preferred_element_type=f32).astype(bf16)

    def post(step, sender):
        return pltpu.make_async_remote_copy(
            src_ref=outbox.at[step],
            dst_ref=inbox.at[sender],
            send_sem=box_send.at[step],
            recv_sem=box_recv.at[sender],
            device_id=(row, lax.rem(me + step, n)),
            device_id_type=MESH,
        )

    @pl.loop(1, n)
    def _(step):
        dest = lax.rem(me + step, n)
        ask(step, dest).wait_recv()
        outbox[step] = picked(dest)
        post(step, me).start()

    inbox[me] = picked(me)

    @pl.loop(n // 2, n)
    def _(j):
        mix_block(j)

    acc[...] = jnp.dot(inbox[me], mix[me], preferred_element_type=f32)

    @pl.loop(1, n)
    def _(step):
        sender = lax.rem(me - step + n, n)
        post(step, sender).wait_recv()
        acc[...] += jnp.dot(inbox[sender], mix[sender], preferred_element_type=f32)

    grid = acc[...].T.reshape(tile_rows, blocks, HALO, 2 * FIELDS)
    for xb in range(blocks):
        pad[xb + 1, edge : edge + inner, :] = (
            grid[:, xb].reshape(inner, 2 * FIELDS).astype(bf16)
        )

    @pl.when(jnp.logical_not(has_up))
    def _():
        pad[:, :edge] = jnp.zeros((blocks + 2, edge, 2 * FIELDS), bf16)

    @pl.when(jnp.logical_not(has_down))
    def _():
        pad[:, edge + inner :] = jnp.zeros((blocks + 2, edge, 2 * FIELDS), bf16)

    mid = slice(edge, edge + inner)
    first, last = slice(edge, 2 * edge), slice(inner, inner + edge)
    low, high = slice(0, edge), slice(edge + inner, 2 * edge + inner)
    every = slice(1, blocks + 1)
    left, right = slice(1, 2), slice(blocks, blocks + 1)
    before, after = slice(0, 1), slice(blocks + 1, blocks + 2)
    moves = [
        (0, 1, (right, mid), (before, mid)),
        (0, -1, (left, mid), (after, mid)),
        (1, 0, (every, last), (every, low)),
        (1, 1, (right, last), (before, low)),
        (1, -1, (left, last), (after, low)),
        (-1, 0, (every, first), (every, high)),
        (-1, 1, (right, first), (before, high)),
        (-1, -1, (left, first), (after, high)),
    ]

    def shift(i):
        dr, dc, src, dst = moves[i]
        return pltpu.make_async_remote_copy(
            src_ref=pad.at[src[0], src[1]],
            dst_ref=pad.at[dst[0], dst[1]],
            send_sem=halo_send.at[i],
            recv_sem=halo_recv.at[i],
            device_id=(row + dr, lax.rem(me + dc + n, n)),
            device_id_type=MESH,
        )

    @pl.when(has_down)
    def _():
        for i in (2, 3, 4):
            shift(i).start()

    @pl.when(has_up)
    def _():
        for i in (5, 6, 7):
            shift(i).start()

    for i in (0, 1):
        shift(i).start()
    for i in (0, 1):
        shift(i).wait()

    @pl.when(has_up)
    def _():
        for i in (2, 3, 4):
            shift(i).wait_recv()

    @pl.when(has_down)
    def _():
        for i in (5, 6, 7):
            shift(i).wait_recv()

    parts = [
        pad[xb].astype(f32).reshape(tile_rows + 2 * HALO, HALO, 2 * FIELDS)
        for xb in range(blocks + 2)
    ]
    out_ref[...] = jnp.concatenate(parts, axis=1).reshape(out_ref.shape).astype(bf16)

    @pl.when(has_down)
    def _():
        for i in (2, 3, 4):
            shift(i).wait_send()

    @pl.when(has_up)
    def _():
        for i in (5, 6, 7):
            shift(i).wait_send()

    @pl.loop(1, n)
    def _(step):
        ask(step, me).wait_send()
        post(step, me).wait_send()


def regrid(source, wanted, stencil, weight, tile_rows, tile_cols):
    f32, bf16 = jnp.float32, jnp.bfloat16
    n, cap = wanted.shape
    cells, columns = source.shape
    spots = tile_rows * tile_cols
    blocks = tile_cols // HALO
    rows = tile_rows + 2 * HALO
    dma = pltpu.SemaphoreType.DMA
    return pl.pallas_call(
        functools.partial(regrid_kernel, tile_rows, tile_cols),
        out_shape=jax.ShapeDtypeStruct((rows * (tile_cols + 2 * HALO), columns), bf16),
        in_specs=[pl.BlockSpec(memory_space=pltpu.VMEM)] * 4,
        out_specs=pl.BlockSpec(memory_space=pltpu.VMEM),
        scratch_shapes=[
            pltpu.VMEM((n, n, cap), jnp.int32),
            pltpu.VMEM((columns, cells), bf16),
            pltpu.VMEM((n, cap, spots), bf16),
            pltpu.VMEM((n, columns, cap), bf16),
            pltpu.VMEM((n, columns, cap), bf16),
            pltpu.VMEM((columns, spots), f32),
            pltpu.VMEM((blocks + 2, rows * HALO, columns), bf16),
            dma((n,)), dma((n,)), dma((n,)), dma((n,)), dma((8,)), dma((8,)),
        ],
        compiler_params=pltpu.CompilerParams(
            collective_id=0, has_side_effects=True, vmem_limit_bytes=40 * 1024 * 1024
        ),
        cost_estimate=pl.CostEstimate(
            flops=10**9, bytes_accessed=2 * 10**6, transcendentals=0
        ),
    )(source, wanted, stencil, weight)


def body(source_tiles, requests, stencil, regrid_weight, *weights):
    tile_rows, tile_cols, taps = stencil.shape
    cells, columns = source_tiles.shape[2:]
    padded = regrid(
        source_tiles.reshape(cells, columns),
        requests.reshape(requests.shape[2:]),
        stencil.transpose(2, 0, 1).reshape(taps, -1),
        regrid_weight.transpose(2, 0, 1).reshape(taps, -1),
        tile_rows,
        tile_cols,
    )
    result = unet(padded, tile_rows, tile_cols, weights)
    return result.reshape(tile_rows, tile_cols, 2, FIELDS)


def solution(mesh):
    placed = (P("row", "col", None, None),) * 2 + (P("row", "col", None),) * 2 + (P(),) * 7
    return jax.shard_map(
        body, mesh=mesh, in_specs=placed, out_specs=P("row", "col", None, None), check_vma=False
    )
```

```python
import functools

import jax
import jax.numpy as jnp
from jax import lax
from jax.experimental import pallas as pl
from jax.experimental.pallas import tpu as pltpu
from jax.sharding import PartitionSpec as P

FIELDS = 64
CH = 128
HALO = 8


def silu(a):
    return a * (0.5 + 0.5 * jnp.tanh(0.5 * a))


def unet_kernel(
    tile_rows, tile_cols, p_ref, w_in, w_enc, w_m1, w_m2, w_d1, w_d2, w_out, out_ref,
    first, skip, pooled, middle, up, dec1, tmp, c_in, c_enc, c_m1, c_m2, c_d1, c_d2, c_out, pairs,
):
    wide = tile_cols + 2 * HALO
    half = wide // 2
    row = lax.axis_index("row")
    at_top = row == 0
    at_bottom = row == lax.axis_size("row") - 1
    f32, bf16 = jnp.float32, jnp.bfloat16

    c_in[...] = jnp.zeros_like(c_in)
    c_out[...] = jnp.zeros_like(c_out)
    w_last = w_out[...].astype(f32).T.astype(bf16)
    for b in range(2):
        c_out[b * CH : (b + 1) * CH, b * FIELDS : (b + 1) * FIELDS] = w_last
    size = p_ref.shape[0]
    values = p_ref[...].astype(f32)
    turned = pltpu.roll(values, FIELDS, 1)
    below = pltpu.roll(values, size - wide, 0)
    turned_below = pltpu.roll(turned, size - wide, 0)
    low = lax.broadcasted_iota(jnp.int32, (size, CH), 1) < FIELDS
    pairs[0] = jnp.where(low, values, turned_below).astype(bf16)
    pairs[1] = jnp.where(low, turned, below).astype(bf16)
    for dy in range(3):
        for dx in range(3):
            rows = slice(dy * CH, (dy + 1) * CH)
            cols = slice(dx * CH, (dx + 1) * CH)
            c_in[dy * FIELDS : (dy + 1) * FIELDS, cols] = w_in[dy, dx]
            c_enc[rows, cols] = w_enc[dy, dx]
            c_m1[rows, cols] = w_m1[dy, dx]
            c_m2[rows, cols] = w_m2[dy, dx]
            c_d1[rows, cols] = w_d1[dy, dx, :CH]
            c_d1[(dy + 3) * CH : (dy + 4) * CH, cols] = w_d1[dy, dx, CH:]
            c_d2[rows, cols] = w_d2[dy, dx]

    def conv(sources, weight, width, chunk_rows, start, steps=(0, 1, 2)):
        size = chunk_rows * width
        windows = [
            load(pl.multiple_of(start + (offset + dy) * width, 8), size).astype(bf16)
            for load, offset in sources
            for dy in steps
        ]
        u = jnp.dot(jnp.concatenate(windows, axis=1), weight[...], preferred_element_type=f32)
        return silu(
            u[:, CH : 2 * CH]
            + pltpu.roll(u[:, :CH], 1, 0)
            + pltpu.roll(u[:, 2 * CH :], size - 1, 0)
        )

    def per_chunk(height, chunk_rows, width, step):
        chunks = height // chunk_rows

        @pl.loop(0, 2 * chunks)
        def _(i):
            b = i // chunks
            start = pl.multiple_of((i % chunks) * (chunk_rows * width), 8)
            step(b, start)

    def clear(ref, depth, inner, width):
        @pl.when(at_top)
        def _():
            ref[:, : depth * width] = jnp.zeros((2, depth * width, CH), ref.dtype)

        @pl.when(at_bottom)
        def _():
            ref[:, (depth + inner) * width :] = jnp.zeros((2, depth * width, CH), ref.dtype)

    def reader(ref, b):
        return lambda start, size: ref[b, pl.ds(start, size), :]

    h_first = tile_rows + 14
    h_skip = tile_rows + 12
    h_pool = h_skip // 2
    h_mid = h_pool - 2
    h_coarse = h_mid - 2
    h_dec1 = tile_rows + 2

    def first_step(b, start):
        chunk = h_first // 2
        value = conv([(reader(pairs, b), 0)], c_in, wide, chunk, start, (0, 2))
        first[b, pl.ds(start, chunk * wide), :] = value.astype(bf16)

    per_chunk(h_first, h_first // 2, wide, first_step)
    clear(first, 7, tile_rows, wide)

    def skip_step(b, start):
        chunk = h_skip // 2
        value = conv([(reader(first, b), 0)], c_enc, wide, chunk, start)
        skip[b, pl.ds(start, chunk * wide), :] = value.astype(bf16)

    per_chunk(h_skip, h_skip // 2, wide, skip_step)
    clear(skip, 6, tile_rows, wide)

    @pl.loop(0, 2)
    def _(b):
        s = skip[b].astype(f32).reshape(h_pool, 2 * wide, CH)
        tmp[: h_pool * wide, :] = (s[:, :wide] + s[:, wide:]).reshape(h_pool * wide, CH)
        total = (
            tmp[pl.ds(0, h_pool * half, stride=2), :] + tmp[pl.ds(1, h_pool * half, stride=2), :]
        )
        pooled[b] = (total * 0.25).astype(bf16).astype(f32)

    def mid_step(b, start):
        value = conv([(reader(pooled, b), 0)], c_m1, half, h_mid, start)
        middle[b, pl.ds(start, h_mid * half), :] = value.astype(bf16).astype(f32)

    per_chunk(h_mid, h_mid, half, mid_step)
    clear(middle, 2, tile_rows // 2, half)

    @pl.loop(0, 2)
    def _(b):
        value = conv([(reader(middle, b), 0)], c_m2, half, h_coarse, 0)
        size = h_coarse * half
        tmp[pl.ds(0, size, stride=2), :] = value
        tmp[pl.ds(1, size, stride=2), :] = value
        v = tmp[: h_coarse * wide, :].astype(bf16).reshape(h_coarse, 1, wide, CH)
        up[b] = jnp.broadcast_to(v, (h_coarse, 2, wide, CH)).reshape(2 * h_coarse * wide, CH)

    clear(up, 2, tile_rows, wide)

    def dec1_step(b, start):
        chunk = h_dec1 // 2
        value = conv([(reader(up, b), 0), (reader(skip, b), 4)], c_d1, wide, chunk, start)
        dec1[b, pl.ds(start, chunk * wide), :] = value.astype(bf16)

    per_chunk(h_dec1, h_dec1 // 2, wide, dec1_step)
    clear(dec1, 1, tile_rows, wide)

    chunk = tile_rows // 2

    @pl.loop(0, 2)
    def _(i):
        start = pl.multiple_of(i * (chunk * wide), 8)
        both = []
        for b in range(2):
            value = conv([(reader(dec1, b), 0)], c_d2, wide, chunk, start)
            value = value.reshape(chunk, wide, CH)[:, HALO : HALO + tile_cols]
            both.append(value.reshape(chunk * tile_cols, CH).astype(bf16))
        result = jnp.dot(
            jnp.concatenate(both, axis=1), c_out[...], preferred_element_type=f32
        )
        place = pl.multiple_of(i * (chunk * tile_cols), 8)
        out_ref[pl.ds(place, chunk * tile_cols), :] = result.astype(bf16)


def unet(padded, tile_rows, tile_cols, weights):
    wide = tile_cols + 2 * HALO
    half = wide // 2
    f32, bf16 = jnp.float32, jnp.bfloat16
    square = pltpu.VMEM((3 * CH, 3 * CH), bf16)
    scratch = [
        pltpu.VMEM((2, (tile_rows + 14) * wide, CH), bf16),
        pltpu.VMEM((2, (tile_rows + 12) * wide, CH), bf16),
        pltpu.VMEM((2, (tile_rows // 2 + 6) * half, CH), f32),
        pltpu.VMEM((2, (tile_rows // 2 + 4) * half, CH), f32),
        pltpu.VMEM((2, (tile_rows + 4) * wide, CH), bf16),
        pltpu.VMEM((2, (tile_rows + 2) * wide, CH), bf16),
        pltpu.VMEM(((tile_rows // 2 + 6) * wide, CH), f32),
        pltpu.VMEM((4 * FIELDS, 3 * CH), bf16),
        square, square, square,
        pltpu.VMEM((6 * CH, 3 * CH), bf16),
        square,
        pltpu.VMEM((2 * CH, 2 * FIELDS), bf16),
        pltpu.VMEM((2, (tile_rows + 2 * HALO) * wide, CH), bf16),
    ]
    return pl.pallas_call(
        functools.partial(unet_kernel, tile_rows, tile_cols),
        out_shape=jax.ShapeDtypeStruct((tile_rows * tile_cols, 2 * FIELDS), bf16),
        in_specs=[pl.BlockSpec(memory_space=pltpu.VMEM)] * 8,
        out_specs=pl.BlockSpec(memory_space=pltpu.VMEM),
        scratch_shapes=scratch,
        compiler_params=pltpu.CompilerParams(vmem_limit_bytes=44 * 1024 * 1024),
        cost_estimate=pl.CostEstimate(
            flops=6 * 10**9, bytes_accessed=4 * 10**6, transcendentals=2 * 10**6
        ),
    )(padded, *weights[:-1], weights[-1].T)


MESH = pl.DeviceIdType.MESH


def regrid_kernel(
    tile_rows, tile_cols, src_ref, req_ref, sten_ref, wgt_ref, out_ref,
    reqs, src_t, mix, outbox, inbox, acc, pad, slot_rows, weight_rows,
    req_send, req_recv, box_send, box_recv, halo_send, halo_recv,
):
    f32, bf16 = jnp.float32, jnp.bfloat16
    row, me = lax.axis_index("row"), lax.axis_index("col")
    n_row, n = lax.axis_size("row"), lax.axis_size("col")
    cap = req_ref.shape[1]
    cells = src_ref.shape[0]
    spots = tile_rows * tile_cols
    has_up, has_down = row > 0, row < n_row - 1
    blocks = tile_cols // HALO
    edge = HALO * HALO
    inner = tile_rows * HALO

    barrier = pltpu.get_barrier_semaphore()

    def greet(r, c):
        pl.semaphore_signal(
            barrier, inc=1, device_id=(r, lax.rem(c + n, n)), device_id_type=MESH
        )

    @pl.loop(1, n)
    def _(step):
        greet(row, me + step)

    @pl.when(has_up)
    def _():
        for d in (-1, 0, 1):
            greet(row - 1, me + d)

    @pl.when(has_down)
    def _():
        for d in (-1, 0, 1):
            greet(row + 1, me + d)

    rows_beside = jnp.minimum(row, 1) + jnp.minimum(n_row - 1 - row, 1)
    pl.semaphore_wait(barrier, n - 1 + 3 * rows_beside)

    def ask(step, sender):
        return pltpu.make_async_remote_copy(
            src_ref=req_ref,
            dst_ref=reqs.at[sender],
            send_sem=req_send.at[step],
            recv_sem=req_recv.at[sender],
            device_id=(row, lax.rem(me + step, n)),
            device_id_type=MESH,
        )

    @pl.loop(1, n)
    def _(step):
        ask(step, me).start()

    reqs[me] = req_ref[...]
    src_t[...] = src_ref[...].astype(f32).T.astype(bf16)

    taps = sten_ref.shape[1]
    for k in range(taps):
        slot_rows[k : k + 1, :] = jnp.concatenate(
            [sten_ref[y, k : k + 1, :] for y in range(tile_rows)], axis=1
        ).astype(f32)
        weight_rows[k : k + 1, :] = jnp.concatenate(
            [wgt_ref[y, k : k + 1, :] for y in range(tile_rows)], axis=1
        )
    piece = 256

    def hits(values, base, width):
        ids = lax.broadcasted_iota(jnp.int32, (piece, width), 0).astype(f32).astype(bf16)
        near = jnp.broadcast_to(values - jnp.asarray(base, jnp.int32).astype(f32), (piece, width))
        return ids == near.astype(bf16)

    def mix_block(j):
        for start in range(0, cap, piece):
            total = None
            for k in range(taps):
                hit = hits(slot_rows[k : k + 1, :], j * cap + start, spots)
                weight = jnp.broadcast_to(weight_rows[k : k + 1, :], (piece, spots)).astype(bf16)
                part = jnp.where(hit, weight, jnp.zeros((), bf16))
                total = part if total is None else total + part
            mix[j, start : start + piece] = total

    @pl.loop(0, n // 2)
    def _(j):
        mix_block(j)

    def picked(dest):
        asked = reqs[dest, pl.ds(me, 1), :].astype(f32)
        hot = jnp.concatenate(
            [
                jnp.where(hits(asked, start, cap), jnp.ones((), bf16), jnp.zeros((), bf16))
                for start in range(0, cells, piece)
            ],
            axis=0,
        )
        return jnp.dot(src_t[...], hot, preferred_element_type=f32).astype(bf16)

    def post(step, sender):
        return pltpu.make_async_remote_copy(
            src_ref=outbox.at[step],
            dst_ref=inbox.at[sender],
            send_sem=box_send.at[step],
            recv_sem=box_recv.at[sender],
            device_id=(row, lax.rem(me + step, n)),
            device_id_type=MESH,
        )

    @pl.loop(1, n)
    def _(step):
        dest = lax.rem(me + step, n)
        ask(step, dest).wait_recv()
        outbox[step] = picked(dest)
        post(step, me).start()

    inbox[me] = picked(me)

    @pl.loop(n // 2, n)
    def _(j):
        mix_block(j)

    acc[...] = jnp.dot(inbox[me], mix[me], preferred_element_type=f32)

    @pl.loop(1, n)
    def _(step):
        sender = lax.rem(me - step + n, n)
        post(step, sender).wait_recv()
        acc[...] += jnp.dot(inbox[sender], mix[sender], preferred_element_type=f32)

    grid = acc[...].T.reshape(tile_rows, blocks, HALO, 2 * FIELDS)
    for xb in range(blocks):
        pad[xb + 1, edge : edge + inner, :] = (
            grid[:, xb].reshape(inner, 2 * FIELDS).astype(bf16)
        )

    @pl.when(jnp.logical_not(has_up))
    def _():
        pad[:, :edge] = jnp.zeros((blocks + 2, edge, 2 * FIELDS), bf16)

    @pl.when(jnp.logical_not(has_down))
    def _():
        pad[:, edge + inner :] = jnp.zeros((blocks + 2, edge, 2 * FIELDS), bf16)

    mid = slice(edge, edge + inner)
    first, last = slice(edge, 2 * edge), slice(inner, inner + edge)
    low, high = slice(0, edge), slice(edge + inner, 2 * edge + inner)
    every = slice(1, blocks + 1)
    left, right = slice(1, 2), slice(blocks, blocks + 1)
    before, after = slice(0, 1), slice(blocks + 1, blocks + 2)
    moves = [
        (0, 1, (right, mid), (before, mid)),
        (0, -1, (left, mid), (after, mid)),
        (1, 0, (every, last), (every, low)),
        (1, 1, (right, last), (before, low)),
        (1, -1, (left, last), (after, low)),
        (-1, 0, (every, first), (every, high)),
        (-1, 1, (right, first), (before, high)),
        (-1, -1, (left, first), (after, high)),
    ]

    def shift(i):
        dr, dc, src, dst = moves[i]
        return pltpu.make_async_remote_copy(
            src_ref=pad.at[src[0], src[1]],
            dst_ref=pad.at[dst[0], dst[1]],
            send_sem=halo_send.at[i],
            recv_sem=halo_recv.at[i],
            device_id=(row + dr, lax.rem(me + dc + n, n)),
            device_id_type=MESH,
        )

    @pl.when(has_down)
    def _():
        for i in (2, 3, 4):
            shift(i).start()

    @pl.when(has_up)
    def _():
        for i in (5, 6, 7):
            shift(i).start()

    for i in (0, 1):
        shift(i).start()
    for i in (0, 1):
        shift(i).wait()

    @pl.when(has_up)
    def _():
        for i in (2, 3, 4):
            shift(i).wait_recv()

    @pl.when(has_down)
    def _():
        for i in (5, 6, 7):
            shift(i).wait_recv()

    parts = [
        pad[xb].astype(f32).reshape(tile_rows + 2 * HALO, HALO, 2 * FIELDS)
        for xb in range(blocks + 2)
    ]
    out_ref[...] = jnp.concatenate(parts, axis=1).reshape(out_ref.shape).astype(bf16)

    @pl.when(has_down)
    def _():
        for i in (2, 3, 4):
            shift(i).wait_send()

    @pl.when(has_up)
    def _():
        for i in (5, 6, 7):
            shift(i).wait_send()

    @pl.loop(1, n)
    def _(step):
        ask(step, me).wait_send()
        post(step, me).wait_send()


def regrid(source, wanted, stencil, weight, tile_rows, tile_cols):
    f32, bf16 = jnp.float32, jnp.bfloat16
    n, cap = wanted.shape
    cells, columns = source.shape
    spots = tile_rows * tile_cols
    blocks = tile_cols // HALO
    rows = tile_rows + 2 * HALO
    dma = pltpu.SemaphoreType.DMA
    return pl.pallas_call(
        functools.partial(regrid_kernel, tile_rows, tile_cols),
        out_shape=jax.ShapeDtypeStruct((rows * (tile_cols + 2 * HALO), columns), bf16),
        in_specs=[pl.BlockSpec(memory_space=pltpu.VMEM)] * 4,
        out_specs=pl.BlockSpec(memory_space=pltpu.VMEM),
        scratch_shapes=[
            pltpu.VMEM((n, n, cap), jnp.int32),
            pltpu.VMEM((columns, cells), bf16),
            pltpu.VMEM((n, cap, spots), bf16),
            pltpu.VMEM((n, columns, cap), bf16),
            pltpu.VMEM((n, columns, cap), bf16),
            pltpu.VMEM((columns, spots), f32),
            pltpu.VMEM((blocks + 2, rows * HALO, columns), bf16),
            pltpu.VMEM((stencil.shape[1], spots), f32),
            pltpu.VMEM((stencil.shape[1], spots), f32),
            dma((n,)), dma((n,)), dma((n,)), dma((n,)), dma((8,)), dma((8,)),
        ],
        compiler_params=pltpu.CompilerParams(
            collective_id=0, has_side_effects=True, vmem_limit_bytes=40 * 1024 * 1024
        ),
        cost_estimate=pl.CostEstimate(
            flops=10**9, bytes_accessed=2 * 10**6, transcendentals=0
        ),
    )(source, wanted, stencil, weight)


def body(source_tiles, requests, stencil, regrid_weight, *weights):
    tile_rows, tile_cols = stencil.shape[:2]
    cells, columns = source_tiles.shape[2:]
    padded = regrid(
        source_tiles.reshape(cells, columns),
        requests.reshape(requests.shape[2:]),
        stencil.transpose(0, 2, 1),
        regrid_weight.transpose(0, 2, 1),
        tile_rows,
        tile_cols,
    )
    result = unet(padded, tile_rows, tile_cols, weights)
    return result.reshape(tile_rows, tile_cols, 2, FIELDS)


def solution(mesh):
    placed = (P("row", "col", None, None),) * 2 + (P("row", "col", None),) * 2 + (P(),) * 7
    return jax.shard_map(
        body, mesh=mesh, in_specs=placed, out_specs=P("row", "col", None, None), check_vma=False
    )
```

```python
import functools

import jax
import jax.numpy as jnp
from jax import lax
from jax.experimental import pallas as pl
from jax.experimental.pallas import tpu as pltpu
from jax.sharding import PartitionSpec as P

FIELDS = 64
CH = 128
HALO = 8


def silu(a):
    return a * (0.5 + 0.5 * jnp.tanh(0.5 * a))


def unet_kernel(
    tile_rows, tile_cols, p_ref, w_in, w_enc, w_m1, w_m2, w_d1, w_d2, w_out, out_ref,
    first, skip, pooled, middle, up, dec1, tmp, c_in, c_enc, c_m1, c_m2, c_d1, c_d2, c_out, pairs,
):
    wide = tile_cols + 2 * HALO
    half = wide // 2
    row = lax.axis_index("row")
    at_top = row == 0
    at_bottom = row == lax.axis_size("row") - 1
    f32, bf16 = jnp.float32, jnp.bfloat16

    c_in[...] = jnp.zeros_like(c_in)
    c_out[...] = jnp.zeros_like(c_out)
    w_last = w_out[...].astype(f32).T.astype(bf16)
    for b in range(2):
        c_out[b * CH : (b + 1) * CH, b * FIELDS : (b + 1) * FIELDS] = w_last
    size = p_ref.shape[0]
    values = p_ref[...].astype(f32)
    turned = pltpu.roll(values, FIELDS, 1)
    below = pltpu.roll(values, size - wide, 0)
    turned_below = pltpu.roll(turned, size - wide, 0)
    low = lax.broadcasted_iota(jnp.int32, (size, CH), 1) < FIELDS
    pairs[0] = jnp.where(low, values, turned_below).astype(bf16)
    pairs[1] = jnp.where(low, turned, below).astype(bf16)
    for dy in range(3):
        for dx in range(3):
            rows = slice(dy * CH, (dy + 1) * CH)
            cols = slice(dx * CH, (dx + 1) * CH)
            c_in[dy * FIELDS : (dy + 1) * FIELDS, cols] = w_in[dy, dx]
            c_enc[rows, cols] = w_enc[dy, dx]
            c_m1[rows, cols] = w_m1[dy, dx]
            c_m2[rows, cols] = w_m2[dy, dx]
            c_d1[rows, cols] = w_d1[dy, dx, :CH]
            c_d1[(dy + 3) * CH : (dy + 4) * CH, cols] = w_d1[dy, dx, CH:]
            c_d2[rows, cols] = w_d2[dy, dx]

    def conv(sources, weight, width, chunk_rows, start, steps=(0, 1, 2)):
        size = chunk_rows * width
        windows = [
            load(pl.multiple_of(start + (offset + dy) * width, 8), size).astype(bf16)
            for load, offset in sources
            for dy in steps
        ]
        u = jnp.dot(jnp.concatenate(windows, axis=1), weight[...], preferred_element_type=f32)
        return silu(
            u[:, CH : 2 * CH]
            + pltpu.roll(u[:, :CH], 1, 0)
            + pltpu.roll(u[:, 2 * CH :], size - 1, 0)
        )

    def per_chunk(height, chunk_rows, width, step):
        chunks = height // chunk_rows

        @pl.loop(0, 2 * chunks)
        def _(i):
            b = i // chunks
            start = pl.multiple_of((i % chunks) * (chunk_rows * width), 8)
            step(b, start)

    def clear(ref, depth, inner, width):
        @pl.when(at_top)
        def _():
            ref[:, : depth * width] = jnp.zeros((2, depth * width, CH), ref.dtype)

        @pl.when(at_bottom)
        def _():
            ref[:, (depth + inner) * width :] = jnp.zeros((2, depth * width, CH), ref.dtype)

    def reader(ref, b):
        return lambda start, size: ref[b, pl.ds(start, size), :]

    h_first = tile_rows + 14
    h_skip = tile_rows + 12
    h_pool = h_skip // 2
    h_mid = h_pool - 2
    h_coarse = h_mid - 2
    h_dec1 = tile_rows + 2

    def first_step(b, start):
        chunk = h_first // 2
        value = conv([(reader(pairs, b), 0)], c_in, wide, chunk, start, (0, 2))
        first[b, pl.ds(start, chunk * wide), :] = value.astype(bf16)

    per_chunk(h_first, h_first // 2, wide, first_step)
    clear(first, 7, tile_rows, wide)

    def skip_step(b, start):
        chunk = h_skip // 2
        value = conv([(reader(first, b), 0)], c_enc, wide, chunk, start)
        skip[b, pl.ds(start, chunk * wide), :] = value.astype(bf16)

    per_chunk(h_skip, h_skip // 2, wide, skip_step)
    clear(skip, 6, tile_rows, wide)

    @pl.loop(0, 2)
    def _(b):
        s = skip[b].astype(f32).reshape(h_pool, 2 * wide, CH)
        tmp[: h_pool * wide, :] = (s[:, :wide] + s[:, wide:]).reshape(h_pool * wide, CH)
        total = (
            tmp[pl.ds(0, h_pool * half, stride=2), :] + tmp[pl.ds(1, h_pool * half, stride=2), :]
        )
        pooled[b] = (total * 0.25).astype(bf16).astype(f32)

    def mid_step(b, start):
        value = conv([(reader(pooled, b), 0)], c_m1, half, h_mid, start)
        middle[b, pl.ds(start, h_mid * half), :] = value.astype(bf16).astype(f32)

    per_chunk(h_mid, h_mid, half, mid_step)
    clear(middle, 2, tile_rows // 2, half)

    @pl.loop(0, 2)
    def _(b):
        value = conv([(reader(middle, b), 0)], c_m2, half, h_coarse, 0)
        size = h_coarse * half
        tmp[pl.ds(0, size, stride=2), :] = value
        tmp[pl.ds(1, size, stride=2), :] = value
        v = tmp[: h_coarse * wide, :].astype(bf16).reshape(h_coarse, 1, wide, CH)
        up[b] = jnp.broadcast_to(v, (h_coarse, 2, wide, CH)).reshape(2 * h_coarse * wide, CH)

    clear(up, 2, tile_rows, wide)

    def dec1_step(b, start):
        chunk = h_dec1 // 2
        value = conv([(reader(up, b), 0), (reader(skip, b), 4)], c_d1, wide, chunk, start)
        dec1[b, pl.ds(start, chunk * wide), :] = value.astype(bf16)

    per_chunk(h_dec1, h_dec1 // 2, wide, dec1_step)
    clear(dec1, 1, tile_rows, wide)

    chunk = tile_rows // 2

    @pl.loop(0, 2)
    def _(i):
        start = pl.multiple_of(i * (chunk * wide), 8)
        both = []
        for b in range(2):
            value = conv([(reader(dec1, b), 0)], c_d2, wide, chunk, start)
            value = value.reshape(chunk, wide, CH)[:, HALO : HALO + tile_cols]
            both.append(value.reshape(chunk * tile_cols, CH).astype(bf16))
        result = jnp.dot(
            jnp.concatenate(both, axis=1), c_out[...], preferred_element_type=f32
        )
        place = pl.multiple_of(i * (chunk * tile_cols), 8)
        out_ref[pl.ds(place, chunk * tile_cols), :] = result.astype(bf16)


def unet(padded, tile_rows, tile_cols, weights):
    wide = tile_cols + 2 * HALO
    half = wide // 2
    f32, bf16 = jnp.float32, jnp.bfloat16
    square = pltpu.VMEM((3 * CH, 3 * CH), bf16)
    scratch = [
        pltpu.VMEM((2, (tile_rows + 14) * wide, CH), bf16),
        pltpu.VMEM((2, (tile_rows + 12) * wide, CH), bf16),
        pltpu.VMEM((2, (tile_rows // 2 + 6) * half, CH), f32),
        pltpu.VMEM((2, (tile_rows // 2 + 4) * half, CH), f32),
        pltpu.VMEM((2, (tile_rows + 4) * wide, CH), bf16),
        pltpu.VMEM((2, (tile_rows + 2) * wide, CH), bf16),
        pltpu.VMEM(((tile_rows // 2 + 6) * wide, CH), f32),
        pltpu.VMEM((4 * FIELDS, 3 * CH), bf16),
        square, square, square,
        pltpu.VMEM((6 * CH, 3 * CH), bf16),
        square,
        pltpu.VMEM((2 * CH, 2 * FIELDS), bf16),
        pltpu.VMEM((2, (tile_rows + 2 * HALO) * wide, CH), bf16),
    ]
    return pl.pallas_call(
        functools.partial(unet_kernel, tile_rows, tile_cols),
        out_shape=jax.ShapeDtypeStruct((tile_rows * tile_cols, 2 * FIELDS), bf16),
        in_specs=[pl.BlockSpec(memory_space=pltpu.VMEM)] * 8,
        out_specs=pl.BlockSpec(memory_space=pltpu.VMEM),
        scratch_shapes=scratch,
        compiler_params=pltpu.CompilerParams(vmem_limit_bytes=44 * 1024 * 1024),
        cost_estimate=pl.CostEstimate(
            flops=6 * 10**9, bytes_accessed=4 * 10**6, transcendentals=2 * 10**6
        ),
    )(padded, *weights[:-1], weights[-1].T)


MESH = pl.DeviceIdType.MESH


def regrid_kernel(
    tile_rows, tile_cols, src_in, req_in, sten_in, wgt_in, out_ref,
    src_ref, req_ref, sten_ref, wgt_ref, load, reqs, src_t, mix, outbox, inbox, acc, pad, slot_rows, weight_rows,
    req_send, req_recv, box_send, box_recv, halo_send, halo_recv,
):
    f32, bf16 = jnp.float32, jnp.bfloat16
    row, me = lax.axis_index("row"), lax.axis_index("col")
    n_row, n = lax.axis_size("row"), lax.axis_size("col")
    cap = req_ref.shape[1]
    cells = src_ref.shape[0]
    spots = tile_rows * tile_cols
    has_up, has_down = row > 0, row < n_row - 1
    blocks = tile_cols // HALO
    edge = HALO * HALO
    inner = tile_rows * HALO

    loads = [
        pltpu.make_async_copy(outer, held, load.at[i])
        for i, (outer, held) in enumerate(
            [(req_in, req_ref), (src_in, src_ref), (sten_in, sten_ref), (wgt_in, wgt_ref)]
        )
    ]
    for copy in loads:
        copy.start()

    barrier = pltpu.get_barrier_semaphore()

    def greet(r, c):
        pl.semaphore_signal(
            barrier, inc=1, device_id=(r, lax.rem(c + n, n)), device_id_type=MESH
        )

    @pl.loop(1, n)
    def _(step):
        greet(row, me + step)

    @pl.when(has_up)
    def _():
        for d in (-1, 0, 1):
            greet(row - 1, me + d)

    @pl.when(has_down)
    def _():
        for d in (-1, 0, 1):
            greet(row + 1, me + d)

    rows_beside = jnp.minimum(row, 1) + jnp.minimum(n_row - 1 - row, 1)
    pl.semaphore_wait(barrier, n - 1 + 3 * rows_beside)

    loads[0].wait()

    def ask(step, sender):
        return pltpu.make_async_remote_copy(
            src_ref=req_ref,
            dst_ref=reqs.at[sender],
            send_sem=req_send.at[step],
            recv_sem=req_recv.at[sender],
            device_id=(row, lax.rem(me + step, n)),
            device_id_type=MESH,
        )

    @pl.loop(1, n)
    def _(step):
        ask(step, me).start()

    reqs[me] = req_ref[...]
    loads[1].wait()
    src_t[...] = src_ref[...].astype(f32).T.astype(bf16)

    loads[2].wait()
    loads[3].wait()
    taps = sten_ref.shape[1]
    for k in range(taps):
        slot_rows[k : k + 1, :] = jnp.concatenate(
            [sten_ref[y, k : k + 1, :] for y in range(tile_rows)], axis=1
        ).astype(f32)
        weight_rows[k : k + 1, :] = jnp.concatenate(
            [wgt_ref[y, k : k + 1, :] for y in range(tile_rows)], axis=1
        )
    tile, piece = 16, 256

    def ladder(width):
        return lax.broadcasted_iota(jnp.int32, (tile, width), 0).astype(f32).astype(bf16)

    def spread(values):
        return jnp.broadcast_to(values, (tile, values.shape[1])).astype(bf16)

    lanes = min(512, spots)
    zero, one = jnp.zeros((), bf16), jnp.ones((), bf16)

    def mix_block(j):
        for left_lane in range(0, spots, lanes):
            here = slice(left_lane, left_lane + lanes)
            ids = ladder(lanes)
            weights = [spread(weight_rows[k : k + 1, here]) for k in range(taps)]
            for start in range(0, cap, piece):
                base = (j * cap + start).astype(f32)
                near = [spread(slot_rows[k : k + 1, here] - base) for k in range(taps)]
                for g in range(0, min(piece, cap), tile):
                    step_ids = ids + jnp.asarray(g, bf16)
                    total = None
                    for k in range(taps):
                        part = jnp.where(step_ids == near[k], weights[k], zero)
                        total = part if total is None else total + part
                    mix[j, start + g : start + g + tile, here] = total

    @pl.loop(0, n // 2)
    def _(j):
        mix_block(j)

    def picked(dest):
        asked = reqs[dest, pl.ds(me, 1), :].astype(f32)
        ids = ladder(cap)
        rows = []
        for start in range(0, cells, piece):
            near = spread(asked - float(start))
            for g in range(0, piece, tile):
                rows.append(jnp.where(ids + jnp.asarray(g, bf16) == near, one, zero))
        hot = jnp.concatenate(rows, axis=0)
        return jnp.dot(src_t[...], hot, preferred_element_type=f32).astype(bf16)

    def post(step, sender):
        return pltpu.make_async_remote_copy(
            src_ref=outbox.at[step],
            dst_ref=inbox.at[sender],
            send_sem=box_send.at[step],
            recv_sem=box_recv.at[sender],
            device_id=(row, lax.rem(me + step, n)),
            device_id_type=MESH,
        )

    @pl.loop(1, n)
    def _(step):
        dest = lax.rem(me + step, n)
        ask(step, dest).wait_recv()
        outbox[step] = picked(dest)
        post(step, me).start()

    inbox[me] = picked(me)

    @pl.loop(n // 2, n)
    def _(j):
        mix_block(j)

    acc[...] = jnp.dot(inbox[me], mix[me], preferred_element_type=f32)

    @pl.loop(1, n)
    def _(step):
        sender = lax.rem(me - step + n, n)
        post(step, sender).wait_recv()
        acc[...] += jnp.dot(inbox[sender], mix[sender], preferred_element_type=f32)

    grid = acc[...].T.reshape(tile_rows, blocks, HALO, 2 * FIELDS)
    for xb in range(blocks):
        pad[xb + 1, edge : edge + inner, :] = (
            grid[:, xb].reshape(inner, 2 * FIELDS).astype(bf16)
        )

    @pl.when(jnp.logical_not(has_up))
    def _():
        pad[:, :edge] = jnp.zeros((blocks + 2, edge, 2 * FIELDS), bf16)

    @pl.when(jnp.logical_not(has_down))
    def _():
        pad[:, edge + inner :] = jnp.zeros((blocks + 2, edge, 2 * FIELDS), bf16)

    mid = slice(edge, edge + inner)
    first, last = slice(edge, 2 * edge), slice(inner, inner + edge)
    low, high = slice(0, edge), slice(edge + inner, 2 * edge + inner)
    every = slice(1, blocks + 1)
    left, right = slice(1, 2), slice(blocks, blocks + 1)
    before, after = slice(0, 1), slice(blocks + 1, blocks + 2)
    moves = [
        (0, 1, (right, mid), (before, mid)),
        (0, -1, (left, mid), (after, mid)),
        (1, 0, (every, last), (every, low)),
        (1, 1, (right, last), (before, low)),
        (1, -1, (left, last), (after, low)),
        (-1, 0, (every, first), (every, high)),
        (-1, 1, (right, first), (before, high)),
        (-1, -1, (left, first), (after, high)),
    ]

    def shift(i):
        dr, dc, src, dst = moves[i]
        return pltpu.make_async_remote_copy(
            src_ref=pad.at[src[0], src[1]],
            dst_ref=pad.at[dst[0], dst[1]],
            send_sem=halo_send.at[i],
            recv_sem=halo_recv.at[i],
            device_id=(row + dr, lax.rem(me + dc + n, n)),
            device_id_type=MESH,
        )

    @pl.when(has_down)
    def _():
        for i in (2, 3, 4):
            shift(i).start()

    @pl.when(has_up)
    def _():
        for i in (5, 6, 7):
            shift(i).start()

    for i in (0, 1):
        shift(i).start()
    for i in (0, 1):
        shift(i).wait()

    @pl.when(has_up)
    def _():
        for i in (2, 3, 4):
            shift(i).wait_recv()

    @pl.when(has_down)
    def _():
        for i in (5, 6, 7):
            shift(i).wait_recv()

    parts = [
        pad[xb].astype(f32).reshape(tile_rows + 2 * HALO, HALO, 2 * FIELDS)
        for xb in range(blocks + 2)
    ]
    out_ref[...] = jnp.concatenate(parts, axis=1).reshape(out_ref.shape).astype(bf16)

    @pl.when(has_down)
    def _():
        for i in (2, 3, 4):
            shift(i).wait_send()

    @pl.when(has_up)
    def _():
        for i in (5, 6, 7):
            shift(i).wait_send()

    @pl.loop(1, n)
    def _(step):
        ask(step, me).wait_send()
        post(step, me).wait_send()


def regrid(source, wanted, stencil, weight, tile_rows, tile_cols):
    f32, bf16 = jnp.float32, jnp.bfloat16
    n, cap = wanted.shape
    cells, columns = source.shape
    spots = tile_rows * tile_cols
    blocks = tile_cols // HALO
    rows = tile_rows + 2 * HALO
    dma = pltpu.SemaphoreType.DMA
    return pl.pallas_call(
        functools.partial(regrid_kernel, tile_rows, tile_cols),
        out_shape=jax.ShapeDtypeStruct((rows * (tile_cols + 2 * HALO), columns), bf16),
        in_specs=[pl.BlockSpec(memory_space=pltpu.HBM)] * 4,
        out_specs=pl.BlockSpec(memory_space=pltpu.VMEM),
        scratch_shapes=[
            pltpu.VMEM(source.shape, bf16),
            pltpu.VMEM(wanted.shape, jnp.int32),
            pltpu.VMEM(stencil.shape, jnp.int32),
            pltpu.VMEM(weight.shape, f32),
            dma((4,)),
            pltpu.VMEM((n, n, cap), jnp.int32),
            pltpu.VMEM((columns, cells), bf16),
            pltpu.VMEM((n, cap, spots), bf16),
            pltpu.VMEM((n, columns, cap), bf16),
            pltpu.VMEM((n, columns, cap), bf16),
            pltpu.VMEM((columns, spots), f32),
            pltpu.VMEM((blocks + 2, rows * HALO, columns), bf16),
            pltpu.VMEM((stencil.shape[1], spots), f32),
            pltpu.VMEM((stencil.shape[1], spots), f32),
            dma((n,)), dma((n,)), dma((n,)), dma((n,)), dma((8,)), dma((8,)),
        ],
        compiler_params=pltpu.CompilerParams(
            collective_id=0, has_side_effects=True, vmem_limit_bytes=40 * 1024 * 1024
        ),
        cost_estimate=pl.CostEstimate(
            flops=10**9, bytes_accessed=2 * 10**6, transcendentals=0
        ),
    )(source, wanted, stencil, weight)


def body(source_tiles, requests, stencil, regrid_weight, *weights):
    tile_rows, tile_cols = stencil.shape[:2]
    cells, columns = source_tiles.shape[2:]
    padded = regrid(
        source_tiles.reshape(cells, columns),
        requests.reshape(requests.shape[2:]),
        stencil.transpose(0, 2, 1),
        regrid_weight.transpose(0, 2, 1),
        tile_rows,
        tile_cols,
    )
    result = unet(padded, tile_rows, tile_cols, weights)
    return result.reshape(tile_rows, tile_cols, 2, FIELDS)


def solution(mesh):
    placed = (P("row", "col", None, None),) * 2 + (P("row", "col", None),) * 2 + (P(),) * 7
    return jax.shard_map(
        body, mesh=mesh, in_specs=placed, out_specs=P("row", "col", None, None), check_vma=False
    )
```

```python
import functools

import jax
import jax.numpy as jnp
from jax import lax
from jax.experimental import pallas as pl
from jax.experimental.pallas import tpu as pltpu
from jax.sharding import PartitionSpec as P

FIELDS = 64
CH = 128
HALO = 8


def silu(a):
    return a * (0.5 + 0.5 * jnp.tanh(0.5 * a))


def unet_kernel(
    tile_rows, tile_cols, p_ref, w_in, w_enc, w_m1, w_m2, w_d1, w_d2, w_out, out_ref,
    first, skip, pooled, middle, up, dec1, tmp, c_in, c_enc, c_m1, c_m2, c_d1, c_d2, c_out, pairs,
):
    wide = tile_cols + 2 * HALO
    half = wide // 2
    row = lax.axis_index("row")
    at_top = row == 0
    at_bottom = row == lax.axis_size("row") - 1
    f32, bf16 = jnp.float32, jnp.bfloat16

    c_in[...] = jnp.zeros_like(c_in)
    c_out[...] = jnp.zeros_like(c_out)
    w_last = w_out[...].astype(f32).T.astype(bf16)
    for b in range(2):
        c_out[b * CH : (b + 1) * CH, b * FIELDS : (b + 1) * FIELDS] = w_last
    size = p_ref.shape[0]
    values = p_ref[...].astype(f32)
    turned = pltpu.roll(values, FIELDS, 1)
    below = pltpu.roll(values, size - wide, 0)
    turned_below = pltpu.roll(turned, size - wide, 0)
    low = lax.broadcasted_iota(jnp.int32, (size, CH), 1) < FIELDS
    pairs[0] = jnp.where(low, values, turned_below).astype(bf16)
    pairs[1] = jnp.where(low, turned, below).astype(bf16)
    for dy in range(3):
        for dx in range(3):
            rows = slice(dy * CH, (dy + 1) * CH)
            cols = slice(dx * CH, (dx + 1) * CH)
            c_in[dy * FIELDS : (dy + 1) * FIELDS, cols] = w_in[dy, dx]
            c_enc[rows, cols] = w_enc[dy, dx]
            c_m1[rows, cols] = w_m1[dy, dx]
            c_m2[rows, cols] = w_m2[dy, dx]
            c_d1[rows, cols] = w_d1[dy, dx, :CH]
            c_d1[(dy + 3) * CH : (dy + 4) * CH, cols] = w_d1[dy, dx, CH:]
            c_d2[rows, cols] = w_d2[dy, dx]

    def conv(sources, weight, width, chunk_rows, start, steps=(0, 1, 2)):
        size = chunk_rows * width
        windows = [
            load(pl.multiple_of(start + (offset + dy) * width, 8), size).astype(bf16)
            for load, offset in sources
            for dy in steps
        ]
        u = jnp.dot(jnp.concatenate(windows, axis=1), weight[...], preferred_element_type=f32)
        return silu(
            u[:, CH : 2 * CH]
            + pltpu.roll(u[:, :CH], 1, 0)
            + pltpu.roll(u[:, 2 * CH :], size - 1, 0)
        )

    def per_chunk(height, chunk_rows, width, step):
        chunks = height // chunk_rows

        @pl.loop(0, 2 * chunks)
        def _(i):
            b = i // chunks
            start = pl.multiple_of((i % chunks) * (chunk_rows * width), 8)
            step(b, start)

    def clear(ref, depth, inner, width):
        @pl.when(at_top)
        def _():
            ref[:, : depth * width] = jnp.zeros((2, depth * width, CH), ref.dtype)

        @pl.when(at_bottom)
        def _():
            ref[:, (depth + inner) * width :] = jnp.zeros((2, depth * width, CH), ref.dtype)

    def reader(ref, b):
        return lambda start, size: ref[b, pl.ds(start, size), :]

    h_first = tile_rows + 14
    h_skip = tile_rows + 12
    h_pool = h_skip // 2
    h_mid = h_pool - 2
    h_coarse = h_mid - 2
    h_dec1 = tile_rows + 2

    def first_step(b, start):
        chunk = h_first // 2
        value = conv([(reader(pairs, b), 0)], c_in, wide, chunk, start, (0, 2))
        first[b, pl.ds(start, chunk * wide), :] = value.astype(bf16)

    per_chunk(h_first, h_first // 2, wide, first_step)
    clear(first, 7, tile_rows, wide)

    def skip_step(b, start):
        chunk = h_skip // 2
        value = conv([(reader(first, b), 0)], c_enc, wide, chunk, start)
        skip[b, pl.ds(start, chunk * wide), :] = value.astype(bf16)

    per_chunk(h_skip, h_skip // 2, wide, skip_step)
    clear(skip, 6, tile_rows, wide)

    @pl.loop(0, 2)
    def _(b):
        s = skip[b].astype(f32).reshape(h_pool, 2 * wide, CH)
        tmp[: h_pool * wide, :] = (s[:, :wide] + s[:, wide:]).reshape(h_pool * wide, CH)
        total = (
            tmp[pl.ds(0, h_pool * half, stride=2), :] + tmp[pl.ds(1, h_pool * half, stride=2), :]
        )
        pooled[b] = (total * 0.25).astype(bf16).astype(f32)

    def mid_step(b, start):
        value = conv([(reader(pooled, b), 0)], c_m1, half, h_mid, start)
        middle[b, pl.ds(start, h_mid * half), :] = value.astype(bf16).astype(f32)

    per_chunk(h_mid, h_mid, half, mid_step)
    clear(middle, 2, tile_rows // 2, half)

    @pl.loop(0, 2)
    def _(b):
        value = conv([(reader(middle, b), 0)], c_m2, half, h_coarse, 0)
        size = h_coarse * half
        tmp[pl.ds(0, size, stride=2), :] = value
        tmp[pl.ds(1, size, stride=2), :] = value
        v = tmp[: h_coarse * wide, :].astype(bf16).reshape(h_coarse, 1, wide, CH)
        up[b] = jnp.broadcast_to(v, (h_coarse, 2, wide, CH)).reshape(2 * h_coarse * wide, CH)

    clear(up, 2, tile_rows, wide)

    def dec1_step(b, start):
        chunk = h_dec1 // 2
        value = conv([(reader(up, b), 0), (reader(skip, b), 4)], c_d1, wide, chunk, start)
        dec1[b, pl.ds(start, chunk * wide), :] = value.astype(bf16)

    per_chunk(h_dec1, h_dec1 // 2, wide, dec1_step)
    clear(dec1, 1, tile_rows, wide)

    chunk = tile_rows // 2

    @pl.loop(0, 2)
    def _(i):
        start = pl.multiple_of(i * (chunk * wide), 8)
        both = []
        for b in range(2):
            value = conv([(reader(dec1, b), 0)], c_d2, wide, chunk, start)
            value = value.reshape(chunk, wide, CH)[:, HALO : HALO + tile_cols]
            both.append(value.reshape(chunk * tile_cols, CH).astype(bf16))
        result = jnp.dot(
            jnp.concatenate(both, axis=1), c_out[...], preferred_element_type=f32
        )
        place = pl.multiple_of(i * (chunk * tile_cols), 8)
        out_ref[pl.ds(place, chunk * tile_cols), :] = result.astype(bf16)


def unet(padded, tile_rows, tile_cols, weights):
    wide = tile_cols + 2 * HALO
    half = wide // 2
    f32, bf16 = jnp.float32, jnp.bfloat16
    square = pltpu.VMEM((3 * CH, 3 * CH), bf16)
    scratch = [
        pltpu.VMEM((2, (tile_rows + 14) * wide, CH), bf16),
        pltpu.VMEM((2, (tile_rows + 12) * wide, CH), bf16),
        pltpu.VMEM((2, (tile_rows // 2 + 6) * half, CH), f32),
        pltpu.VMEM((2, (tile_rows // 2 + 4) * half, CH), f32),
        pltpu.VMEM((2, (tile_rows + 4) * wide, CH), bf16),
        pltpu.VMEM((2, (tile_rows + 2) * wide, CH), bf16),
        pltpu.VMEM(((tile_rows // 2 + 6) * wide, CH), f32),
        pltpu.VMEM((4 * FIELDS, 3 * CH), bf16),
        square, square, square,
        pltpu.VMEM((6 * CH, 3 * CH), bf16),
        square,
        pltpu.VMEM((2 * CH, 2 * FIELDS), bf16),
        pltpu.VMEM((2, (tile_rows + 2 * HALO) * wide, CH), bf16),
    ]
    return pl.pallas_call(
        functools.partial(unet_kernel, tile_rows, tile_cols),
        out_shape=jax.ShapeDtypeStruct((tile_rows * tile_cols, 2 * FIELDS), bf16),
        in_specs=[pl.BlockSpec(memory_space=pltpu.VMEM)] * 8,
        out_specs=pl.BlockSpec(memory_space=pltpu.VMEM),
        scratch_shapes=scratch,
        compiler_params=pltpu.CompilerParams(vmem_limit_bytes=44 * 1024 * 1024),
        cost_estimate=pl.CostEstimate(
            flops=6 * 10**9, bytes_accessed=4 * 10**6, transcendentals=2 * 10**6
        ),
    )(padded, *weights[:-1], weights[-1].T)


MESH = pl.DeviceIdType.MESH


def regrid_kernel(
    tile_rows, tile_cols, src_in, req_in, sten_in, wgt_in, out_ref,
    src_ref, req_ref, sten_ref, wgt_ref, load, reqs, src_t, mix, outbox, inbox, acc, pad, slot_rows, weight_rows,
    req_send, req_recv, box_send, box_recv, halo_send, halo_recv,
):
    f32, bf16 = jnp.float32, jnp.bfloat16
    row, me = lax.axis_index("row"), lax.axis_index("col")
    n_row, n = lax.axis_size("row"), lax.axis_size("col")
    cap = req_ref.shape[1]
    cells = src_ref.shape[0]
    spots = tile_rows * tile_cols
    has_up, has_down = row > 0, row < n_row - 1
    blocks = tile_cols // HALO
    edge = HALO * HALO
    inner = tile_rows * HALO

    loads = [
        pltpu.make_async_copy(outer, held, load.at[i])
        for i, (outer, held) in enumerate(
            [(req_in, req_ref), (src_in, src_ref), (sten_in, sten_ref), (wgt_in, wgt_ref)]
        )
    ]
    for copy in loads:
        copy.start()

    barrier = pltpu.get_barrier_semaphore()

    def greet(r, c):
        pl.semaphore_signal(
            barrier, inc=1, device_id=(r, lax.rem(c + n, n)), device_id_type=MESH
        )

    @pl.loop(1, n)
    def _(step):
        greet(row, me + step)

    @pl.when(has_up)
    def _():
        for d in (-1, 0, 1):
            greet(row - 1, me + d)

    @pl.when(has_down)
    def _():
        for d in (-1, 0, 1):
            greet(row + 1, me + d)

    rows_beside = jnp.minimum(row, 1) + jnp.minimum(n_row - 1 - row, 1)
    pl.semaphore_wait(barrier, n - 1 + 3 * rows_beside)

    loads[0].wait()

    def ask(step, sender):
        return pltpu.make_async_remote_copy(
            src_ref=req_ref,
            dst_ref=reqs.at[sender],
            send_sem=req_send.at[step],
            recv_sem=req_recv.at[sender],
            device_id=(row, lax.rem(me + step, n)),
            device_id_type=MESH,
        )

    @pl.loop(1, n)
    def _(step):
        ask(step, me).start()

    reqs[me] = req_ref[...]
    loads[1].wait()
    src_t[...] = src_ref[...].astype(f32).T.astype(bf16)

    loads[2].wait()
    loads[3].wait()
    taps = sten_ref.shape[1]
    for k in range(taps):
        slot_rows[k : k + 1, :] = jnp.concatenate(
            [sten_ref[y, k : k + 1, :] for y in range(tile_rows)], axis=1
        ).astype(f32)
        weight_rows[k : k + 1, :] = jnp.concatenate(
            [wgt_ref[y, k : k + 1, :] for y in range(tile_rows)], axis=1
        )
    tile, piece = 16, 256

    def ladder(width):
        return lax.broadcasted_iota(jnp.int32, (tile, width), 0).astype(f32).astype(bf16)

    def spread(values):
        return jnp.broadcast_to(values, (tile, values.shape[1])).astype(bf16)

    lanes = min(512, spots)
    zero, one = jnp.zeros((), bf16), jnp.ones((), bf16)

    def mix_block(j):
        for left_lane in range(0, spots, lanes):
            here = slice(left_lane, left_lane + lanes)
            ids = ladder(lanes)
            weights = [spread(weight_rows[k : k + 1, here]) for k in range(taps)]
            for start in range(0, cap, piece):
                base = (j * cap + start).astype(f32)
                near = [spread(slot_rows[k : k + 1, here] - base) for k in range(taps)]
                for g in range(0, min(piece, cap), tile):
                    step_ids = ids + jnp.asarray(g, bf16)
                    total = None
                    for k in range(taps):
                        part = jnp.where(step_ids == near[k], weights[k], zero)
                        total = part if total is None else total + part
                    mix[j, start + g : start + g + tile, here] = total

    @pl.loop(0, n // 2)
    def _(j):
        mix_block(j)

    def picked(dest):
        asked = reqs[dest, pl.ds(me, 1), :].astype(f32)
        ids = ladder(cap)
        rows = []
        for start in range(0, cells, piece):
            near = spread(asked - float(start))
            for g in range(0, piece, tile):
                rows.append(jnp.where(ids + jnp.asarray(g, bf16) == near, one, zero))
        hot = jnp.concatenate(rows, axis=0)
        return jnp.dot(src_t[...], hot, preferred_element_type=f32).astype(bf16)

    def post(step, sender):
        return pltpu.make_async_remote_copy(
            src_ref=outbox.at[step],
            dst_ref=inbox.at[sender],
            send_sem=box_send.at[step],
            recv_sem=box_recv.at[sender],
            device_id=(row, lax.rem(me + step, n)),
            device_id_type=MESH,
        )

    @pl.loop(1, n)
    def _(step):
        dest = lax.rem(me + step, n)
        ask(step, dest).wait_recv()
        outbox[step] = picked(dest)
        post(step, me).start()

    inbox[me] = picked(me)

    @pl.loop(n // 2, n)
    def _(j):
        mix_block(j)

    acc[...] = jnp.dot(inbox[me], mix[me], preferred_element_type=f32)

    @pl.loop(1, n)
    def _(step):
        sender = lax.rem(me - step + n, n)
        post(step, sender).wait_recv()
        acc[...] += jnp.dot(inbox[sender], mix[sender], preferred_element_type=f32)

    grid = acc[...].T.reshape(tile_rows, blocks, HALO, 2 * FIELDS)
    for xb in range(blocks):
        pad[xb + 1, edge : edge + inner, :] = (
            grid[:, xb].reshape(inner, 2 * FIELDS).astype(bf16)
        )

    @pl.when(jnp.logical_not(has_up))
    def _():
        pad[:, :edge] = jnp.zeros((blocks + 2, edge, 2 * FIELDS), bf16)

    @pl.when(jnp.logical_not(has_down))
    def _():
        pad[:, edge + inner :] = jnp.zeros((blocks + 2, edge, 2 * FIELDS), bf16)

    mid = slice(edge, edge + inner)
    first, last = slice(edge, 2 * edge), slice(inner, inner + edge)
    low, high = slice(0, edge), slice(edge + inner, 2 * edge + inner)
    every = slice(1, blocks + 1)
    left, right = slice(1, 2), slice(blocks, blocks + 1)
    before, after = slice(0, 1), slice(blocks + 1, blocks + 2)
    moves = [
        (0, 1, (right, mid), (before, mid)),
        (0, -1, (left, mid), (after, mid)),
        (1, 0, (every, last), (every, low)),
        (1, 1, (right, last), (before, low)),
        (1, -1, (left, last), (after, low)),
        (-1, 0, (every, first), (every, high)),
        (-1, 1, (right, first), (before, high)),
        (-1, -1, (left, first), (after, high)),
    ]

    def shift(i):
        dr, dc, src, dst = moves[i]
        return pltpu.make_async_remote_copy(
            src_ref=pad.at[src[0], src[1]],
            dst_ref=pad.at[dst[0], dst[1]],
            send_sem=halo_send.at[i],
            recv_sem=halo_recv.at[i],
            device_id=(row + dr, lax.rem(me + dc + n, n)),
            device_id_type=MESH,
        )

    @pl.when(has_down)
    def _():
        for i in (2, 3, 4):
            shift(i).start()

    @pl.when(has_up)
    def _():
        for i in (5, 6, 7):
            shift(i).start()

    for i in (0, 1):
        shift(i).start()
    for i in (0, 1):
        shift(i).wait()

    @pl.when(has_up)
    def _():
        for i in (2, 3, 4):
            shift(i).wait_recv()

    @pl.when(has_down)
    def _():
        for i in (5, 6, 7):
            shift(i).wait_recv()

    parts = [
        pad[xb].astype(f32).reshape(tile_rows + 2 * HALO, HALO, 2 * FIELDS)
        for xb in range(blocks + 2)
    ]
    out_ref[...] = jnp.concatenate(parts, axis=1).reshape(out_ref.shape).astype(bf16)

    @pl.when(has_down)
    def _():
        for i in (2, 3, 4):
            shift(i).wait_send()

    @pl.when(has_up)
    def _():
        for i in (5, 6, 7):
            shift(i).wait_send()

    @pl.loop(1, n)
    def _(step):
        ask(step, me).wait_send()
        post(step, me).wait_send()


def regrid(source, wanted, stencil, weight, tile_rows, tile_cols):
    f32, bf16 = jnp.float32, jnp.bfloat16
    n, cap = wanted.shape
    cells, columns = source.shape
    spots = tile_rows * tile_cols
    blocks = tile_cols // HALO
    rows = tile_rows + 2 * HALO
    dma = pltpu.SemaphoreType.DMA
    return pl.pallas_call(
        functools.partial(regrid_kernel, tile_rows, tile_cols),
        out_shape=jax.ShapeDtypeStruct((rows * (tile_cols + 2 * HALO), columns), bf16),
        in_specs=[pl.BlockSpec(memory_space=pltpu.HBM)] * 4,
        out_specs=pl.BlockSpec(memory_space=pltpu.VMEM),
        scratch_shapes=[
            pltpu.VMEM(source.shape, bf16),
            pltpu.VMEM(wanted.shape, jnp.int32),
            pltpu.VMEM(stencil.shape, jnp.int32),
            pltpu.VMEM(weight.shape, f32),
            dma((4,)),
            pltpu.VMEM((n, n, cap), jnp.int32),
            pltpu.VMEM((columns, cells), bf16),
            pltpu.VMEM((n, cap, spots), bf16),
            pltpu.VMEM((n, columns, cap), bf16),
            pltpu.VMEM((n, columns, cap), bf16),
            pltpu.VMEM((columns, spots), f32),
            pltpu.VMEM((blocks + 2, rows * HALO, columns), bf16),
            pltpu.VMEM((stencil.shape[1], spots), f32),
            pltpu.VMEM((stencil.shape[1], spots), f32),
            dma((n,)), dma((n,)), dma((n,)), dma((n,)), dma((8,)), dma((8,)),
        ],
        compiler_params=pltpu.CompilerParams(
            collective_id=0, has_side_effects=True, vmem_limit_bytes=56 * 1024 * 1024
        ),
        cost_estimate=pl.CostEstimate(
            flops=10**9, bytes_accessed=2 * 10**6, transcendentals=0
        ),
    )(source, wanted, stencil, weight)


def body(source_tiles, requests, stencil, regrid_weight, *weights):
    tile_rows, tile_cols = stencil.shape[:2]
    cells, columns = source_tiles.shape[2:]
    padded = regrid(
        source_tiles.reshape(cells, columns),
        requests.reshape(requests.shape[2:]),
        stencil.transpose(0, 2, 1),
        regrid_weight.transpose(0, 2, 1),
        tile_rows,
        tile_cols,
    )
    result = unet(padded, tile_rows, tile_cols, weights)
    return result.reshape(tile_rows, tile_cols, 2, FIELDS)


def solution(mesh):
    placed = (P("row", "col", None, None),) * 2 + (P("row", "col", None),) * 2 + (P(),) * 7
    return jax.shard_map(
        body, mesh=mesh, in_specs=placed, out_specs=P("row", "col", None, None), check_vma=False
    )
```
